512 devices in a mesh: seq: 32 (over z, x), req: 8 (over y), chan: 2 (over core).
Axes of the slice: x: 4, y: 8, z: 8, core: 2. Of those that a mesh axis runs over, the one named last changes fastest.
Arguments:
- context: bfloat16 [8, 4096, 4096], P('req', 'chan', 'seq'), may hold values from -6 to 6
- filters: bfloat16 [4096, 8192], P('chan', 'seq'), may hold values from -0.09375 to 0.09375
- lengths: int32 [8], replicated, may hold values from 131072 to 524288, as said below
Outputs:
- future: bfloat16 [8, 4096, 4096], P('req', 'chan', 'seq')
The draws below stay inside these ranges and needn't reach their ends.
Inputs may be any that keep to these rules, and one draw needn't show every extreme that they name: `lengths`: exactly 4 of the 8 requests have a length that is a multiple of 4096; how many of them fall on one index of req differs between indices.
All inputs are finite; a program needn't handle non-finite values.
Results may differ from the reference program's by a relative error of at most 0.0078.
Values may be sent and summed in bfloat16 or wider, within the bound.
No kernel may reach another device: no remote copies, remote signals or barrier semaphores. Data moves between devices by JAX's collectives and lax.ppermute only.
A program may use at most 64 MiB of HBM per device.

```python
import math
import jax
import jax.numpy as jnp
from jax import lax

D = 4096
B = 4096
RQ = 1
REQS = 8
DUE = 4
N_SEQ = 32


def draw_lengths(key, part):
    key = jax.random.fold_in(key, 7)
    key_heat, key_score, key_base, key_tail = jax.random.split(key, 4)
    group_count = REQS // RQ
    heat = jax.random.randint(key_heat, (group_count,), 0, 4)
    owner_group = jnp.arange(REQS, dtype=jnp.int32) // RQ
    noise = jax.random.randint(key_score, (REQS,), 0, 4096)
    scores = (heat[owner_group] * 4096 + noise) * REQS + jnp.arange(REQS, dtype=jnp.int32)
    order = jnp.argsort(-scores)
    places = jnp.zeros((REQS,), jnp.int32).at[order].set(jnp.arange(REQS, dtype=jnp.int32))
    due_mask = places < DUE
    blocks_done = jax.random.randint(key_base, (REQS,), 32, 129)
    blocks_done = blocks_done.at[order[DUE - 1]].set(32)
    blocks_done = blocks_done.at[order[0]].set(128)
    tail_count = jax.random.randint(key_tail, (REQS,), 1, B)
    partial_len = jnp.minimum(blocks_done, 127) * B + tail_count
    return jnp.where(due_mask, blocks_done * B, partial_len).astype(jnp.int32)


def shard_levels(rng, shape, cuts, low, high):
    gain, own = 1.0, jax.random.fold_in(rng, 6)
    for position, blocks in cuts:
        steps = jnp.exp(jax.random.uniform(jax.random.fold_in(own, position), (blocks,), jnp.float32, low / len(cuts), high / len(cuts)))
        gain = gain * jnp.repeat(steps, shape[position] // blocks).reshape([-1 if axis == position else 1 for axis in range(len(shape))])
    return gain


def normal_values(stream_key, dims, deviation, bound, cuts=(), kind=jnp.bfloat16):
    level = shard_levels(stream_key, dims, cuts, -0.22, 0.18) if cuts else 1.0
    entries = jax.random.normal(stream_key, dims, jnp.float32) * deviation * level
    return jnp.minimum(jnp.maximum(entries, -bound), bound).astype(kind)


def setup_inputs(seed: int = 0) -> dict:
    key_list = jax.random.split(jax.random.key(seed), 4)
    context = normal_values(key_list[0], (REQS, D, B), 1.0, 6.0, ((0, 8), (1, 2), (2, 32)))
    filters = normal_values(key_list[1], (D, 2 * B), B ** -0.5, 0.09375, ((0, 2), (1, 32)))
    lengths = draw_lengths(jax.random.fold_in(key_list[3], 71), 0)
    return dict(context=context, filters=filters, lengths=lengths)


def trig_pair(first_count, second_count, stride_len, full_len):
    left_index = lax.broadcasted_iota(jnp.int32, (first_count, second_count), 0)
    right_index = lax.broadcasted_iota(jnp.int32, (first_count, second_count), 1)
    phases = (left_index * right_index * stride_len) % full_len
    angles = phases.astype(jnp.float32) * (2.0 * math.pi / full_len)
    return jnp.cos(angles), jnp.sin(angles)


def trig_tables(row_count, col_count):
    full_len = row_count * col_count
    cos_rows, sin_rows = trig_pair(row_count, row_count, col_count, full_len)
    cos_turn, sin_turn = trig_pair(row_count, col_count, 1, full_len)
    cos_cols, sin_cols = trig_pair(col_count, col_count, row_count, full_len)
    return (cos_rows.astype(jnp.bfloat16), sin_rows.astype(jnp.bfloat16), cos_turn, sin_turn,
            cos_cols.astype(jnp.bfloat16), sin_cols.astype(jnp.bfloat16))


def mat_cols(left_part, table):
    return jnp.einsum("...kq,qm->...km", left_part.astype(jnp.float32), table.astype(jnp.float32))


def mat_rows(table, right_part):
    return jnp.einsum("kp,...pq->...kq", table.astype(jnp.float32), right_part.astype(jnp.float32))


def forward_spectrum(signal, trig):
    cos_rows, sin_rows, cos_turn, sin_turn, cos_cols, sin_cols = trig
    used_rows = signal.shape[-2]
    head_real = mat_rows(cos_rows[:, :used_rows], signal)
    head_imag = -mat_rows(sin_rows[:, :used_rows], signal)
    turn_real = (head_real * cos_turn + head_imag * sin_turn).astype(jnp.bfloat16)
    turn_imag = (head_imag * cos_turn - head_real * sin_turn).astype(jnp.bfloat16)
    spec_real = mat_cols(turn_real, cos_cols) + mat_cols(turn_imag, sin_cols)
    spec_imag = mat_cols(turn_imag, cos_cols) - mat_cols(turn_real, sin_cols)
    return spec_real, spec_imag


def future_block(signal, filter_spec, trig):
    cos_rows, sin_rows, cos_turn, sin_turn, cos_cols, sin_cols = trig
    spec_real, spec_imag = forward_spectrum(signal, trig)
    filt_real, filt_imag = filter_spec
    scale_inv = 1.0 / (cos_rows.shape[0] * cos_cols.shape[0])
    prod_real = ((spec_real * filt_real - spec_imag * filt_imag) * scale_inv).astype(jnp.bfloat16)
    prod_imag = ((spec_real * filt_imag + spec_imag * filt_real) * scale_inv).astype(jnp.bfloat16)
    back_real = mat_cols(prod_real, cos_cols) - mat_cols(prod_imag, sin_cols)
    back_imag = mat_cols(prod_real, sin_cols) + mat_cols(prod_imag, cos_cols)
    turn_real = (back_real * cos_turn - back_imag * sin_turn).astype(jnp.bfloat16)
    turn_imag = (back_real * sin_turn + back_imag * cos_turn).astype(jnp.bfloat16)
    half_rows = cos_rows.shape[0] // 2
    tail_real = mat_rows(cos_rows[half_rows:], turn_real)
    tail_imag = mat_rows(sin_rows[half_rows:], turn_imag)
    return (tail_real - tail_imag).astype(jnp.bfloat16)


def reference(context, filters, lengths):
    row_count = 2 * N_SEQ
    col_count = B // N_SEQ
    trig = trig_tables(row_count, col_count)
    due_mask = (lengths % B) == 0
    due_rank = (jnp.cumsum(due_mask.astype(jnp.int32)) - 1).astype(jnp.int32)
    slot_index = lax.broadcasted_iota(jnp.int32, (DUE, REQS), 0)
    req_index = lax.broadcasted_iota(jnp.int32, (DUE, REQS), 1)
    matches = (due_rank[None, :] == slot_index) & due_mask[None, :]
    chosen_rows = jnp.sum(jnp.where(matches, req_index, 0), axis=1).astype(jnp.int32)
    width_block = 128

    def one_slab(offset):
        channel_slab = lax.dynamic_slice_in_dim(context, offset, width_block, 1)
        chosen = jnp.take(channel_slab, chosen_rows, axis=0)
        filter_taps = lax.dynamic_slice_in_dim(filters, offset, width_block, 0)
        filter_spec = forward_spectrum(filter_taps.reshape(width_block, row_count, col_count), trig)
        signal = chosen.reshape(DUE, width_block, row_count // 2, col_count)
        return future_block(signal, filter_spec, trig).reshape(DUE, width_block, B)

    offsets = (jnp.arange(D // width_block) * width_block).astype(jnp.int32)
    slabs = lax.map(one_slab, offsets)
    computed = jnp.transpose(slabs, (1, 0, 2, 3)).reshape(DUE, D, B)
    placed = jnp.take(computed, jnp.clip(due_rank, 0, DUE - 1), axis=0)
    return jnp.where(due_mask[:, None, None], placed, jnp.zeros_like(placed))
```

```python
import functools
import math

import jax
import jax.numpy as jnp
import numpy as np
from jax import lax
from jax.experimental import pallas as pl
from jax.experimental.pallas import tpu as pltpu
from jax.sharding import Mesh, PartitionSpec as P

B = 4096
C8 = 8


def trig_pair(first_count, second_count, stride_len, full_len):
    left = np.arange(first_count)[:, None]
    right = np.arange(second_count)[None, :]
    phases = (left * right * stride_len) % full_len
    angles = phases.astype(np.float64) * (2.0 * math.pi / full_len)
    return np.cos(angles).astype(np.float32), np.sin(angles).astype(np.float32)


def tables(rows, cols):
    full = rows * cols
    bf16 = jnp.bfloat16
    cp, sp = trig_pair(rows, rows, cols, full)
    ct, st = trig_pair(rows, cols, 1, full)
    cq, sq = trig_pair(cols, cols, rows, full)
    eye = np.eye(C8, dtype=np.float32)
    row_fwd = np.kron(np.concatenate([cp, -sp], 0), eye)
    half = rows // 2
    row_inv = np.kron(np.concatenate([cp[half:], -sp[half:]], 1), eye)
    col_fwd = np.block([[cq, -sq], [sq, cq]])
    col_inv = np.block([[cq, sq], [-sq, cq]])
    return (
        row_fwd.astype(bf16),
        row_inv.astype(bf16),
        col_fwd.astype(bf16),
        col_inv.astype(bf16),
        np.repeat(ct, C8, axis=0),
        np.repeat(st, C8, axis=0),
    )


def dot(a, b):
    return jnp.dot(a, b, preferred_element_type=jnp.float32)


def local_kernel(due_ref, got_ref, row_fwd, row_inv, col_fwd, col_inv, turn_cos, turn_sin, out_ref):
    seq, pair, rows, q = got_ref.shape
    chans = out_ref.shape[2]
    kc = turn_cos.shape[0]
    own = chans // pair
    scale = 1.0 / (2 * seq * q)
    ct, st = turn_cos[...], turn_sin[...]
    zero = jnp.zeros((seq, C8, q), jnp.float32)

    def spectrum(head):
        re, im = head[:kc], head[kc:]
        turned = jnp.concatenate(
            [
                (re * ct + im * st).astype(jnp.bfloat16),
                (im * ct - re * st).astype(jnp.bfloat16),
            ],
            1,
        )
        return dot(turned, col_fwd[...])

    def rows_of(part):
        return part.astype(jnp.float32).reshape(-1, q).astype(jnp.bfloat16)

    for group in range(chans // C8):
        holder, place = divmod(group * C8, own)
        first = chans + 2 * place
        taps = rows_of(got_ref[:, holder, first : first + 2 * C8, :])
        filt = spectrum(dot(row_fwd[...], taps)) * scale
        f_re, f_im = filt[:, :q], filt[:, q:]
        signal = jnp.concatenate(
            [rows_of(got_ref[:, b, group * C8 : (group + 1) * C8, :]) for b in range(pair)], 1
        )
        head = dot(row_fwd[:, : seq * C8], signal)
        back = []
        for b in range(pair):
            spec = spectrum(head[:, b * q : (b + 1) * q])
            s_re, s_im = spec[:, :q], spec[:, q:]
            prod = jnp.concatenate(
                [
                    (s_re * f_re - s_im * f_im).astype(jnp.bfloat16),
                    (s_re * f_im + s_im * f_re).astype(jnp.bfloat16),
                ],
                1,
            )
            u = dot(prod, col_inv[...])
            u_re, u_im = u[:, :q], u[:, q:]
            back.append(
                jnp.concatenate(
                    [
                        (u_re * ct - u_im * st).astype(jnp.bfloat16),
                        (u_re * st + u_im * ct).astype(jnp.bfloat16),
                    ],
                    0,
                )
            )
        tail = dot(row_inv[...], jnp.concatenate(back, 1))
        for b in range(pair):
            value = tail[:, b * q : (b + 1) * q].reshape(seq, C8, q)
            value = jnp.where(due_ref[b] == 0, value, zero)
            out_ref[:, b, group * C8 : (group + 1) * C8, :] = value.astype(jnp.bfloat16)


def per_device(consts, pair, context, filters, lengths):
    seq = lax.axis_size("seq")
    chans_all, q = context.shape[1], context.shape[2]
    peers = seq * pair
    chans = chans_all // peers
    own = chans // pair
    low = lax.axis_index("low")
    first = lax.axis_index("high") * pair
    left_over = lax.dynamic_slice_in_dim(lengths % B, first, pair)

    ctx = context.reshape(peers, chans, q)
    mine = lax.dynamic_index_in_dim(filters.reshape(peers, pair, own, 2 * q), low, 1, keepdims=False)
    parts = [ctx]
    for place in range(0, own, C8):
        for half in range(2):
            parts.append(mine[:, place : place + C8, half * q : (half + 1) * q])
    sent = jnp.concatenate(parts, 1)
    got = lax.all_to_all(sent, ("seq", "low"), split_axis=0, concat_axis=0)
    vmem = pl.BlockSpec(memory_space=pltpu.VMEM)
    out = pl.pallas_call(
        local_kernel,
        out_shape=jax.ShapeDtypeStruct((seq, pair, chans, q), jnp.bfloat16),
        in_specs=[pl.BlockSpec(memory_space=pltpu.SMEM)] + [vmem] * 7,
        out_specs=vmem,
        compiler_params=pltpu.CompilerParams(vmem_limit_bytes=48 << 20),
        name="transform",
    )(left_over, got.reshape(seq, pair, chans + 2 * own, q), *consts)
    home = lax.all_to_all(out.reshape(peers, chans, q), ("seq", "low"), split_axis=0, concat_axis=0)
    return home.reshape(context.shape)


def solution(mesh):
    seq, req, chan = (mesh.shape[a] for a in ("seq", "req", "chan"))
    pair = 2
    split = Mesh(mesh.devices.reshape(seq, req // pair, pair, chan), ("seq", "high", "low", "chan"))
    consts = tables(2 * seq, B // seq)
    spec = P(("high", "low"), "chan", "seq")
    return jax.shard_map(
        functools.partial(per_device, consts, pair),
        mesh=split,
        in_specs=(spec, P("chan", "seq"), P()),
        out_specs=spec,
        check_vma=False,
    )
```

```python
import functools
import math

import jax
import jax.numpy as jnp
import numpy as np
from jax import lax
from jax.experimental import pallas as pl
from jax.experimental.pallas import tpu as pltpu
from jax.sharding import Mesh, PartitionSpec as P

B = 4096
C8 = 8


def trig_pair(first_count, second_count, stride_len, full_len):
    left = np.arange(first_count)[:, None]
    right = np.arange(second_count)[None, :]
    phases = (left * right * stride_len) % full_len
    angles = phases.astype(np.float64) * (2.0 * math.pi / full_len)
    return np.cos(angles).astype(np.float32), np.sin(angles).astype(np.float32)


def tables(rows, cols):
    full = rows * cols
    cp, sp = trig_pair(rows, rows, cols, full)
    ct, st = trig_pair(rows, cols, 1, full)
    cq, sq = trig_pair(cols, cols, rows, full)
    eye = np.eye(C8, dtype=np.float32)
    half = rows // 2
    row_fwd = np.kron(np.concatenate([cp, -sp], 0), eye)
    row_inv = np.concatenate([np.kron(cp[half:], eye), np.kron(-sp[half:], eye)], 0)
    col = np.concatenate([np.block([[cq, -sq], [sq, cq]]), np.block([[cq, sq], [-sq, cq]])], 1)
    bands = np.concatenate([row_fwd, row_inv, col], 0).astype(jnp.bfloat16)
    turn = np.repeat(np.concatenate([ct, st], 1), C8, axis=0)
    return bands, turn


def dot(a, b):
    return jnp.dot(a, b, preferred_element_type=jnp.float32)


def pack_kernel(low_ref, context_ref, filters_ref, sent_ref, sems):
    chans, q = context_ref.shape[1:]
    own = filters_ref.shape[2]
    low = low_ref[0]
    copies = [pltpu.make_async_copy(context_ref, sent_ref.at[:, pl.ds(0, chans), :], sems.at[0])]
    for half in range(2):
        copies.append(
            pltpu.make_async_copy(
                filters_ref.at[:, low, :, pl.ds(half * q, q)],
                sent_ref.at[:, pl.ds(chans + half * own, own), :],
                sems.at[1 + half],
            )
        )
    for copy in copies:
        copy.start()
    for copy in copies:
        copy.wait()


def local_kernel(due_ref, got_ref, bands_ref, turn_ref, out_ref):
    seq, pair, rows, q = got_ref.shape
    chans = out_ref.shape[2]
    own = chans // pair
    kc = turn_ref.shape[0]
    row_fwd = bands_ref.at[pl.ds(0, 2 * kc), :]
    row_inv = bands_ref.at[pl.ds(2 * kc, kc), :]
    col = bands_ref.at[pl.ds(3 * kc, 2 * q), :]
    groups = chans // C8
    scale = 1.0 / (2 * seq * q)
    ct, st = turn_ref[:, :q], turn_ref[:, q:]
    zero = jnp.zeros((seq, C8, q), jnp.float32)

    def narrow(part):
        return part.astype(jnp.bfloat16)

    def spectrum(head):
        re, im = head[:kc], head[kc:]
        turned = jnp.concatenate([narrow(re * ct + im * st), narrow(im * ct - re * st)], 1)
        return dot(turned, col[:, : 2 * q])

    taps = []
    for group in range(groups):
        holder, place = divmod(group * C8, own)
        halves = [
            got_ref[:, holder, chans + half * own + place : chans + half * own + place + C8, :].astype(jnp.float32)
            for half in range(2)
        ]
        taps.append(narrow(jnp.stack(halves, 1).reshape(2 * seq * C8, q)))
    filt = []
    for group in range(0, groups, 2):
        head = dot(row_fwd[...], jnp.concatenate(taps[group : group + 2], 1))
        for k in range(2):
            filt.append(spectrum(head[:, k * q : (k + 1) * q]) * scale)

    for group in range(groups):
        f_re, f_im = filt[group][:, :q], filt[group][:, q:]
        lanes = pl.ds(group * C8, C8)
        signal = [narrow(got_ref[:, b, lanes, :].astype(jnp.float32).reshape(seq * C8, q)) for b in range(pair)]
        head = dot(row_fwd[:, : seq * C8], jnp.concatenate(signal, 1))
        back_re, back_im = [], []
        for b in range(pair):
            spec = spectrum(head[:, b * q : (b + 1) * q])
            s_re, s_im = spec[:, :q], spec[:, q:]
            prod = jnp.concatenate([narrow(s_re * f_re - s_im * f_im), narrow(s_re * f_im + s_im * f_re)], 1)
            u = dot(prod, col[:, 2 * q :])
            u_re, u_im = u[:, :q], u[:, q:]
            back_re.append(narrow(u_re * ct - u_im * st))
            back_im.append(narrow(u_re * st + u_im * ct))
        half = seq * C8
        tail = dot(row_inv[:half], jnp.concatenate(back_re, 1)) + dot(row_inv[half:], jnp.concatenate(back_im, 1))
        for b in range(pair):
            value = tail[:, b * q : (b + 1) * q].reshape(seq, C8, q)
            value = jnp.where(due_ref[b] == 0, value, zero)
            out_ref[:, b, lanes, :] = narrow(value)


def per_device(consts, pair, context, filters, lengths):
    seq = lax.axis_size("seq")
    chans_all, q = context.shape[1], context.shape[2]
    peers = seq * pair
    chans = chans_all // peers
    own = chans // pair
    rows = chans + 2 * own
    low = lax.axis_index("low")
    first = lax.axis_index("high") * pair
    left_over = lax.dynamic_slice_in_dim(lengths % B, first, pair)
    smem = pl.BlockSpec(memory_space=pltpu.SMEM)
    vmem = pl.BlockSpec(memory_space=pltpu.VMEM)
    anyw = pl.BlockSpec(memory_space=pl.ANY)

    sent = pl.pallas_call(
        pack_kernel,
        out_shape=jax.ShapeDtypeStruct((peers, rows, q), jnp.bfloat16),
        in_specs=[smem, anyw, anyw],
        out_specs=anyw,
        scratch_shapes=[pltpu.SemaphoreType.DMA((3,))],
        name="pack",
    )(low[None], context.reshape(peers, chans, q), filters.reshape(peers, pair, own, 2 * q))
    got = lax.all_to_all(sent, ("seq", "low"), split_axis=0, concat_axis=0)
    out = pl.pallas_call(
        local_kernel,
        out_shape=jax.ShapeDtypeStruct((seq, pair, chans, q), jnp.bfloat16),
        in_specs=[smem] + [vmem] * 3,
        out_specs=vmem,
        compiler_params=pltpu.CompilerParams(vmem_limit_bytes=48 << 20),
        name="transform",
    )(left_over, got.reshape(seq, pair, rows, q), *consts)
    home = lax.all_to_all(out.reshape(peers, chans, q), ("seq", "low"), split_axis=0, concat_axis=0)
    return home.reshape(context.shape)


def solution(mesh):
    seq, req, chan = (mesh.shape[a] for a in ("seq", "req", "chan"))
    pair = 2
    split = Mesh(mesh.devices.reshape(seq, req // pair, pair, chan), ("seq", "high", "low", "chan"))
    consts = tables(2 * seq, B // seq)
    spec = P(("high", "low"), "chan", "seq")
    return jax.shard_map(
        functools.partial(per_device, consts, pair),
        mesh=split,
        in_specs=(spec, P("chan", "seq"), P()),
        out_specs=spec,
        check_vma=False,
    )
```

```python
import functools
import math

import jax
import jax.numpy as jnp
import numpy as np
from jax import lax
from jax.experimental import pallas as pl
from jax.experimental.pallas import tpu as pltpu
from jax.sharding import Mesh, PartitionSpec as P

B = 4096
C8 = 8


def trig_pair(first_count, second_count, stride_len, full_len):
    left = np.arange(first_count)[:, None]
    right = np.arange(second_count)[None, :]
    phases = (left * right * stride_len) % full_len
    angles = phases.astype(np.float64) * (2.0 * math.pi / full_len)
    return np.cos(angles).astype(np.float32), np.sin(angles).astype(np.float32)


def tables(rows, cols):
    full = rows * cols
    half = rows // 2
    cp, sp = trig_pair(rows, rows, cols, full)
    ct, st = trig_pair(rows, cols, 1, full)
    cq, sq = trig_pair(cols, cols, rows, full)
    eye = np.eye(C8, dtype=np.float32)
    row_fwd = np.kron(np.concatenate([cp[: half + 1], -sp[1:half]], 0), eye)
    twice = np.where(np.arange(half + 1) % half == 0, 1.0, 2.0) / full
    back = np.concatenate([cp[half:, : half + 1] * twice, -sp[half:, 1:half] * twice[1:half]], 1)
    row_inv = np.kron(back, eye)
    col = np.concatenate([np.block([[cq, -sq], [sq, cq]]), np.block([[cq, sq], [-sq, cq]])], 1)
    bands = np.concatenate([row_fwd, row_inv, col], 0).astype(jnp.bfloat16)
    turn = np.repeat(np.concatenate([ct, st], 1)[: half + 1], C8, axis=0).astype(np.float32)
    return bands, turn


def dot(a, b):
    return jnp.dot(a, b, preferred_element_type=jnp.float32)


def pack_kernel(low_ref, context_ref, filters_ref, sent_ref):
    chans, q = context_ref.shape[1:]
    own = filters_ref.shape[2]
    sent_ref[:, :chans, :] = context_ref[...]
    for half in range(2):
        sent_ref[:, chans + half * own : chans + (half + 1) * own, :] = filters_ref[:, 0, :, half * q : (half + 1) * q]


def local_kernel(due_ref, got_ref, bands_ref, turn_ref, out_ref):
    seq, pair, rows, q = got_ref.shape
    chans = out_ref.shape[2]
    own = chans // pair
    length = 2 * seq * C8
    kept = turn_ref.shape[0]
    row_fwd = bands_ref.at[pl.ds(0, length), :]
    row_inv = bands_ref.at[pl.ds(length, length // 2), :]
    col = bands_ref.at[pl.ds(length + length // 2, 2 * q), :]
    groups = chans // C8
    ct, st = turn_ref[:, :q], turn_ref[:, q:]
    edge = jnp.zeros((C8, q), jnp.float32)
    zero = jnp.zeros((seq, C8, q), jnp.float32)

    def narrow(part):
        return part.astype(jnp.bfloat16)

    def spectra(head):
        turned = []
        for i in range(head.shape[1] // q):
            part = head[:, i * q : (i + 1) * q]
            re = part[:kept]
            im = jnp.concatenate([edge, part[kept:], edge], 0)
            turned.append(jnp.concatenate([re * ct + im * st, im * ct - re * st], 1))
        return dot(narrow(jnp.concatenate(turned, 0)), col[:, : 2 * q])

    taps = []
    for group in range(groups):
        holder, place = divmod(group * C8, own)
        halves = [
            got_ref[:, holder, chans + half * own + place : chans + half * own + place + C8, :].astype(jnp.float32)
            for half in range(2)
        ]
        taps.append(narrow(jnp.stack(halves, 1).reshape(length, q)))
    filt = []
    for group in range(0, groups, 2):
        both = spectra(dot(row_fwd[...], jnp.concatenate(taps[group : group + 2], 1)))
        filt += [both[:kept], both[kept:]]

    for group in range(groups):
        f_re, f_im = filt[group][:, :q], filt[group][:, q:]
        lanes = pl.ds(group * C8, C8)
        signal = [narrow(got_ref[:, b, lanes, :].astype(jnp.float32).reshape(seq * C8, q)) for b in range(pair)]
        spec = spectra(dot(row_fwd[:, : seq * C8], jnp.concatenate(signal, 1)))
        prod = []
        for b in range(pair):
            s_re, s_im = spec[b * kept : (b + 1) * kept, :q], spec[b * kept : (b + 1) * kept, q:]
            prod.append(jnp.concatenate([s_re * f_re - s_im * f_im, s_re * f_im + s_im * f_re], 1))
        u = dot(narrow(jnp.concatenate(prod, 0)), col[:, 2 * q :])
        back = []
        for b in range(pair):
            u_re, u_im = u[b * kept : (b + 1) * kept, :q], u[b * kept : (b + 1) * kept, q:]
            v_im = u_re * st + u_im * ct
            back.append(jnp.concatenate([u_re * ct - u_im * st, v_im[C8 : kept - C8]], 0))
        tail = dot(row_inv[...], narrow(jnp.concatenate(back, 1)))
        for b in range(pair):
            value = tail[:, b * q : (b + 1) * q].reshape(seq, C8, q)
            value = jnp.where(due_ref[b] == 0, value, zero)
            out_ref[:, b, lanes, :] = narrow(value)


def per_device(consts, pair, context, filters, lengths):
    seq = lax.axis_size("seq")
    chans_all, q = context.shape[1], context.shape[2]
    peers = seq * pair
    chans = chans_all // peers
    own = chans // pair
    rows = chans + 2 * own
    low = lax.axis_index("low")
    first = lax.axis_index("high") * pair
    left_over = lax.dynamic_slice_in_dim(lengths % B, first, pair)
    smem = pl.BlockSpec(memory_space=pltpu.SMEM)
    vmem = pl.BlockSpec(memory_space=pltpu.VMEM)

    steps = 2
    part = peers // steps
    sent = pl.pallas_call(
        pack_kernel,
        out_shape=jax.ShapeDtypeStruct((peers, rows, q), jnp.bfloat16),
        grid_spec=pltpu.PrefetchScalarGridSpec(
            num_scalar_prefetch=1,
            grid=(steps,),
            in_specs=[
                pl.BlockSpec((part, chans, q), lambda i, low_ref: (i, 0, 0)),
                pl.BlockSpec((part, 1, own, 2 * q), lambda i, low_ref: (i, low_ref[0], 0, 0)),
            ],
            out_specs=pl.BlockSpec((part, rows, q), lambda i, low_ref: (i, 0, 0)),
        ),
        name="pack",
    )(low[None], context.reshape(peers, chans, q), filters.reshape(peers, pair, own, 2 * q))
    got = lax.all_to_all(sent, ("seq", "low"), split_axis=0, concat_axis=0)
    out = pl.pallas_call(
        local_kernel,
        out_shape=jax.ShapeDtypeStruct((seq, pair, chans, q), jnp.bfloat16),
        in_specs=[smem] + [vmem] * 3,
        out_specs=vmem,
        compiler_params=pltpu.CompilerParams(vmem_limit_bytes=48 << 20),
        name="transform",
    )(left_over, got.reshape(seq, pair, rows, q), *consts)
    home = lax.all_to_all(out.reshape(peers, chans, q), ("seq", "low"), split_axis=0, concat_axis=0)
    return home.reshape(context.shape)


def solution(mesh):
    seq, req, chan = (mesh.shape[a] for a in ("seq", "req", "chan"))
    pair = 2
    split = Mesh(mesh.devices.reshape(seq, req // pair, pair, chan), ("seq", "high", "low", "chan"))
    consts = tables(2 * seq, B // seq)
    spec = P(("high", "low"), "chan", "seq")
    return jax.shard_map(
        functools.partial(per_device, consts, pair),
        mesh=split,
        in_specs=(spec, P("chan", "seq"), P()),
        out_specs=spec,
        check_vma=False,
    )
```

```python
import functools
import math

import jax
import jax.numpy as jnp
import numpy as np
from jax import lax
from jax.experimental import pallas as pl
from jax.experimental.pallas import tpu as pltpu
from jax.sharding import PartitionSpec as P

B = 4096
C8 = 8


def trig_pair(first_count, second_count, stride_len, full_len):
    left = np.arange(first_count)[:, None]
    right = np.arange(second_count)[None, :]
    phases = (left * right * stride_len) % full_len
    angles = phases.astype(np.float64) * (2.0 * math.pi / full_len)
    return np.cos(angles).astype(np.float32), np.sin(angles).astype(np.float32)


def tables(rows, cols):
    full = rows * cols
    half = rows // 2
    cp, sp = trig_pair(rows, rows, cols, full)
    ct, st = trig_pair(rows, cols, 1, full)
    cq, sq = trig_pair(cols, cols, rows, full)
    eye = np.eye(C8, dtype=np.float32)
    row_fwd = np.kron(np.concatenate([cp[: half + 1], -sp[1:half]], 0), eye)
    twice = np.where(np.arange(half + 1) % half == 0, 1.0, 2.0) / full
    back = np.concatenate([cp[half:, : half + 1] * twice, -sp[half:, 1:half] * twice[1:half]], 1)
    row_inv = np.kron(back, eye)
    col = np.concatenate([np.block([[cq, -sq], [sq, cq]]), np.block([[cq, sq], [-sq, cq]])], 1)
    bands = np.concatenate([row_fwd, row_inv, col], 0).astype(jnp.bfloat16)
    turn = np.repeat(np.concatenate([ct, st], 1)[: half + 1], C8, axis=0).astype(np.float32)
    return bands, turn


def dot(a, b):
    return jnp.dot(a, b, preferred_element_type=jnp.float32)


def local_kernel(due_ref, context_ref, near_ref, next_ref, far_ref, last_ref, bands_ref, turn_ref, out_ref):
    left_over, part = due_ref[0], due_ref[1]
    seq, parts, chans, q = context_ref.shape
    length = 2 * seq * C8
    kept = turn_ref.shape[0]
    row_fwd = bands_ref.at[pl.ds(0, length), :]
    row_inv = bands_ref.at[pl.ds(length, length // 2), :]
    col = bands_ref.at[pl.ds(length + length // 2, 2 * q), :]
    groups = chans // C8

    def narrow(value):
        return value.astype(jnp.bfloat16)

    def beside(values):
        return narrow(jnp.concatenate(values, 1))

    def below(values):
        return jnp.concatenate(values, 0)

    @pl.when(left_over != 0)
    def _():
        out_ref[...] = jnp.zeros_like(out_ref)

    @pl.when(left_over == 0)
    def _():
        ct, st = turn_ref[:, :q], turn_ref[:, q:]
        edge = jnp.zeros((C8, q), jnp.float32)

        def spectra(head):
            turned = []
            for i in range(groups):
                value = head[:, i * q : (i + 1) * q]
                re = value[:kept]
                im = below([edge, value[kept:], edge])
                turned.append(jnp.concatenate([re * ct + im * st, im * ct - re * st], 1))
            return dot(narrow(below(turned)), col[:, : 2 * q])

        for step, filter_ref in enumerate((near_ref, next_ref, far_ref, last_ref)):
            place = lax.rem(part + step, parts)
            taps, signal = [], []
            for i in range(groups):
                rows = slice(i * C8, (i + 1) * C8)
                halves = [filter_ref[:, rows, h * q : (h + 1) * q].astype(jnp.float32) for h in range(2)]
                taps.append(jnp.stack(halves, 1).reshape(length, q))
                signal.append(context_ref[:, place, rows, :].astype(jnp.float32).reshape(seq * C8, q))
            filt = spectra(dot(row_fwd[...], beside(taps)))
            spec = spectra(dot(row_fwd[:, : seq * C8], beside(signal)))
            f_re, f_im, s_re, s_im = filt[:, :q], filt[:, q:], spec[:, :q], spec[:, q:]
            u = dot(beside([s_re * f_re - s_im * f_im, s_re * f_im + s_im * f_re]), col[:, 2 * q :])
            back = []
            for i in range(groups):
                u_re, u_im = u[i * kept : (i + 1) * kept, :q], u[i * kept : (i + 1) * kept, q:]
                v_im = u_re * st + u_im * ct
                back.append(below([u_re * ct - u_im * st, v_im[C8 : kept - C8]]))
            tail = dot(row_inv[...], beside(back))
            for i in range(groups):
                value = tail[:, i * q : (i + 1) * q].reshape(seq, C8, q)
                out_ref[:, place, i * C8 : (i + 1) * C8, :] = narrow(value)


def per_device(consts, parts, context, filters, lengths):
    seq, reqs = lax.axis_size("seq"), lax.axis_size("req")
    home = lax.axis_index("req")
    part = home % parts
    q = context.shape[2]
    chans = context.shape[1] // seq // parts
    left_over = lax.dynamic_index_in_dim(lengths, home, 0, keepdims=False) % B

    mine = lax.dynamic_index_in_dim(filters.reshape(seq, parts, chans, 2 * q), part, 1, keepdims=False)
    near = lax.all_to_all(mine, "seq", split_axis=0, concat_axis=0)
    context, near = lax.optimization_barrier((context, near))
    got = lax.all_to_all(context.reshape(seq, parts * chans, q), "seq", split_axis=0, concat_axis=0)
    rest = []
    for step in range(1, parts):
        hop = step if 2 * step <= parts else step - parts
        rest.append(lax.ppermute(near, "req", [((r + hop) % reqs, r) for r in range(reqs)]))

    smem = pl.BlockSpec(memory_space=pltpu.SMEM)
    vmem = pl.BlockSpec(memory_space=pltpu.VMEM)
    out = pl.pallas_call(
        local_kernel,
        out_shape=jax.ShapeDtypeStruct((seq, parts, chans, q), jnp.bfloat16),
        in_specs=[smem] + [vmem] * (1 + parts + 2),
        out_specs=vmem,
        compiler_params=pltpu.CompilerParams(vmem_limit_bytes=48 << 20),
        name="transform",
    )(jnp.stack([left_over, part]), got.reshape(seq, parts, chans, q), near, *rest, *consts)
    done = lax.all_to_all(out.reshape(seq, parts * chans, q), "seq", split_axis=0, concat_axis=0)
    return done.reshape(context.shape)


def solution(mesh):
    seq = mesh.shape["seq"]
    parts = 4
    consts = tables(2 * seq, B // seq)
    spec = P("req", "chan", "seq")
    return jax.shard_map(
        functools.partial(per_device, consts, parts),
        mesh=mesh,
        in_specs=(spec, P("chan", "seq"), P()),
        out_specs=spec,
        check_vma=False,
    )
```

```python
import functools
import math

import jax
import jax.numpy as jnp
import numpy as np
from jax import lax
from jax.experimental import pallas as pl
from jax.experimental.pallas import tpu as pltpu
from jax.sharding import PartitionSpec as P

B = 4096
C8 = 8


def trig_pair(first_count, second_count, stride_len, full_len):
    left = np.arange(first_count)[:, None]
    right = np.arange(second_count)[None, :]
    phases = (left * right * stride_len) % full_len
    angles = phases.astype(np.float64) * (2.0 * math.pi / full_len)
    return np.cos(angles).astype(np.float32), np.sin(angles).astype(np.float32)


def tables(rows, cols):
    full = rows * cols
    half = rows // 2
    cp, sp = trig_pair(rows, rows, cols, full)
    ct, st = trig_pair(rows, cols, 1, full)
    cq, sq = trig_pair(cols, cols, rows, full)
    eye = np.eye(C8, dtype=np.float32)
    row_fwd = np.kron(np.concatenate([cp[: half + 1], -sp[1:half]], 0), eye)
    twice = np.where(np.arange(half + 1) % half == 0, 1.0, 2.0) / full
    back = np.concatenate([cp[half:, : half + 1] * twice, -sp[half:, 1:half] * twice[1:half]], 1)
    row_inv = np.kron(back, eye)
    col = np.concatenate([np.block([[cq, -sq], [sq, cq]]), np.block([[cq, sq], [-sq, cq]])], 1)
    bands = np.concatenate([row_fwd, row_inv, col], 0).astype(jnp.bfloat16)
    turn = np.repeat(np.concatenate([ct, st], 1)[: half + 1], C8, axis=0).astype(np.float32)
    return bands, turn


def dot(a, b):
    return jnp.dot(a, b, preferred_element_type=jnp.float32)


PARTNERS = (1, 2, 6, 3, 7, 5, 4)


def pack_kernel(lengths_ref, home_ref, context_ref, filters_ref, sent_ref, plan_ref):
    reqs = lengths_ref.shape[0]
    chans, q = context_ref.shape[1:]
    home = home_ref[0]

    def put(row, group):
        for half in range(2):
            first = row + half * C8
            sent_ref[:, first : first + C8, :] = filters_ref[:, group * C8 : (group + 1) * C8, half * q : (half + 1) * q]

    own_due = lax.rem(lengths_ref[home], B) == 0

    @pl.when(own_due)
    def _():
        sent_ref[:, :chans, :] = context_ref[...]
        put(chans, 0)

    @pl.when(jnp.logical_not(own_due))
    def _():
        for group in range(1, chans // C8):
            put((group - 1) * 2 * C8, group)

    @pl.when(pl.program_id(0) == 0)
    def _():
        due = [jnp.where(lax.rem(lengths_ref[r], B) == 0, 1, 0) for r in range(reqs)]
        choice = jnp.int32(0)
        partner = home ^ PARTNERS[0]
        for i in reversed(range(len(PARTNERS))):
            v = PARTNERS[i]
            clash = functools.reduce(jnp.add, [due[r] * due[r ^ v] for r in range(reqs) if r < r ^ v])
            fits = clash == 0
            choice = jnp.where(fits, i, choice)
            partner = jnp.where(fits, home ^ v, partner)
        first_is_due = jnp.where(home < partner, own_due, jnp.logical_not(own_due))
        plan_ref[0] = choice
        plan_ref[1] = jnp.where(first_is_due, 0, 1)


def local_kernel(plan_ref, got_ref, bands_ref, turn_ref, out_ref):
    side = plan_ref[1]
    seq, _, _, q = got_ref.shape
    chans = out_ref.shape[2]
    length = 2 * seq * C8
    kept = turn_ref.shape[0]
    row_fwd = bands_ref.at[pl.ds(0, length), :]
    row_inv = bands_ref.at[pl.ds(length, length // 2), :]
    col = bands_ref.at[pl.ds(length + length // 2, 2 * q), :]
    ct, st = turn_ref[:, :q], turn_ref[:, q:]
    edge = jnp.zeros((C8, q), jnp.float32)
    wide = 2

    def narrow(value):
        return value.astype(jnp.bfloat16)

    def beside(values):
        return narrow(jnp.concatenate(values, 1))

    def below(values):
        return jnp.concatenate(values, 0)

    def rows_of(at, first, count):
        return got_ref[:, at, first : first + count, :].astype(jnp.float32).reshape(seq * count, q)

    def spectra(head):
        turned = []
        for i in range(wide):
            value = head[:, i * q : (i + 1) * q]
            re = value[:kept]
            im = below([edge, value[kept:], edge])
            turned.append(jnp.concatenate([re * ct + im * st, im * ct - re * st], 1))
        return dot(narrow(below(turned)), col[:, : 2 * q])

    out_ref[:, 1 - side, :, :] = jnp.zeros((seq, chans, q), jnp.bfloat16)
    for first in range(0, chans // C8, wide):
        taps, signal = [], []
        for group in range(first, first + wide):
            if group:
                taps.append(rows_of(1 - side, (group - 1) * 2 * C8, 2 * C8))
            else:
                taps.append(rows_of(side, chans, 2 * C8))
            signal.append(rows_of(side, group * C8, C8))
        filt = spectra(dot(row_fwd[...], beside(taps)))
        spec = spectra(dot(row_fwd[:, : seq * C8], beside(signal)))
        f_re, f_im, s_re, s_im = filt[:, :q], filt[:, q:], spec[:, :q], spec[:, q:]
        u = dot(beside([s_re * f_re - s_im * f_im, s_re * f_im + s_im * f_re]), col[:, 2 * q :])
        back = []
        for i in range(wide):
            u_re, u_im = u[i * kept : (i + 1) * kept, :q], u[i * kept : (i + 1) * kept, q:]
            v_im = u_re * st + u_im * ct
            back.append(below([u_re * ct - u_im * st, v_im[C8 : kept - C8]]))
        tail = dot(row_inv[...], beside(back))
        for i in range(wide):
            value = tail[:, i * q : (i + 1) * q].reshape(seq, C8, q)
            group = first + i
            out_ref[:, side, group * C8 : (group + 1) * C8, :] = narrow(value)


def exchange(choice, value, seq, reqs):
    def paired(v):
        groups = [[s * reqs + side for s in range(seq) for side in (r, r ^ v)] for r in range(reqs) if r < r ^ v]
        return lambda x: lax.all_to_all(x, ("seq", "req"), split_axis=0, concat_axis=0, axis_index_groups=groups)

    return lax.switch(choice, [paired(v) for v in PARTNERS], value)


def per_device(consts, context, filters, lengths):
    seq, reqs = lax.axis_size("seq"), lax.axis_size("req")
    home = lax.axis_index("req")
    q = context.shape[2]
    peers = 2 * seq
    chans = context.shape[1] // peers
    rows = chans + 2 * C8
    smem = pl.BlockSpec(memory_space=pltpu.SMEM)
    vmem = pl.BlockSpec(memory_space=pltpu.VMEM)

    steps = 2
    part = peers // steps
    sent, plan = pl.pallas_call(
        pack_kernel,
        out_shape=[jax.ShapeDtypeStruct((peers, rows, q), jnp.bfloat16), jax.ShapeDtypeStruct((2,), jnp.int32)],
        grid=(steps,),
        in_specs=[
            smem,
            smem,
            pl.BlockSpec((part, chans, q), lambda i: (i, 0, 0)),
            pl.BlockSpec((part, chans, 2 * q), lambda i: (i, 0, 0)),
        ],
        out_specs=[pl.BlockSpec((part, rows, q), lambda i: (i, 0, 0)), smem],
        name="pack",
    )(lengths, home[None], context.reshape(peers, chans, q), filters.reshape(peers, chans, 2 * q))
    got = exchange(plan[0], sent, seq, reqs)
    out = pl.pallas_call(
        local_kernel,
        out_shape=jax.ShapeDtypeStruct((seq, 2, chans, q), jnp.bfloat16),
        in_specs=[smem] + [vmem] * 3,
        out_specs=vmem,
        compiler_params=pltpu.CompilerParams(vmem_limit_bytes=48 << 20),
        name="transform",
    )(plan, got.reshape(seq, 2, rows, q), *consts)
    done = exchange(plan[0], out.reshape(peers, chans, q), seq, reqs)
    return done.reshape(context.shape)


def solution(mesh):
    seq = mesh.shape["seq"]
    consts = tables(2 * seq, B // seq)
    spec = P("req", "chan", "seq")
    return jax.shard_map(
        functools.partial(per_device, consts),
        mesh=mesh,
        in_specs=(spec, P("chan", "seq"), P()),
        out_specs=spec,
        check_vma=False,
    )
```

```python
import functools
import math

import jax
import jax.numpy as jnp
import numpy as np
from jax import lax
from jax.experimental import pallas as pl
from jax.experimental.pallas import tpu as pltpu
from jax.sharding import PartitionSpec as P

B = 4096
C8 = 8


def trig_pair(first_count, second_count, stride_len, full_len):
    left = np.arange(first_count)[:, None]
    right = np.arange(second_count)[None, :]
    phases = (left * right * stride_len) % full_len
    angles = phases.astype(np.float64) * (2.0 * math.pi / full_len)
    return np.cos(angles).astype(np.float32), np.sin(angles).astype(np.float32)


def tables(rows, cols):
    full = rows * cols
    half = rows // 2
    cp, sp = trig_pair(rows, rows, cols, full)
    ct, st = trig_pair(rows, cols, 1, full)
    cq, sq = trig_pair(cols, cols, rows, full)
    eye = np.eye(C8, dtype=np.float32)
    row_fwd = np.kron(np.concatenate([cp[: half + 1], -sp[1:half]], 0), eye)
    twice = np.where(np.arange(half + 1) % half == 0, 1.0, 2.0) / full
    back = np.concatenate([cp[half:, : half + 1] * twice, -sp[half:, 1:half] * twice[1:half]], 1)
    row_inv = np.kron(back, eye)
    col = np.concatenate([np.block([[cq, -sq], [sq, cq]]), np.block([[cq, sq], [-sq, cq]])], 1)
    bands = np.concatenate([row_fwd, row_inv, col], 0).astype(jnp.bfloat16)
    turn = np.repeat(np.concatenate([ct, st], 1)[: half + 1], C8, axis=0).astype(np.float32)
    return bands, turn


def dot(a, b):
    return jnp.dot(a, b, preferred_element_type=jnp.float32)


PAIRINGS = (
    ((0, 1), (2, 3), (4, 5), (6, 7)),
    ((0, 3), (1, 2), (4, 7), (5, 6)),
    ((0, 7), (1, 2), (3, 4), (5, 6)),
    ((0, 7), (1, 6), (2, 5), (3, 4)),
    ((0, 1), (2, 7), (3, 6), (4, 5)),
    ((0, 6), (1, 3), (2, 4), (5, 7)),
    ((0, 2), (1, 7), (3, 5), (4, 6)),
    ((0, 5), (1, 4), (2, 3), (6, 7)),
)


def pack_kernel(lengths_ref, home_ref, context_ref, filters_ref, sent_ref, plan_ref):
    reqs = lengths_ref.shape[0]
    chans, q = context_ref.shape[1:]
    home = home_ref[0]

    def put(row, group):
        for half in range(2):
            first = row + half * C8
            sent_ref[:, first : first + C8, :] = filters_ref[:, group * C8 : (group + 1) * C8, half * q : (half + 1) * q]

    own_due = lax.rem(lengths_ref[home], B) == 0

    @pl.when(own_due)
    def _():
        sent_ref[:, :chans, :] = context_ref[...]
        put(chans, 0)

    @pl.when(jnp.logical_not(own_due))
    def _():
        for group in range(1, chans // C8):
            put((group - 1) * 2 * C8, group)

    @pl.when(pl.program_id(0) == 0)
    def _():
        due = [jnp.where(lax.rem(lengths_ref[r], B) == 0, 1, 0) for r in range(reqs)]
        choice, partners = jnp.int32(0), jnp.int32(0)
        for i in reversed(range(len(PAIRINGS))):
            clash = functools.reduce(jnp.add, [due[a] * due[b] for a, b in PAIRINGS[i]])
            code = sum((b << 4 * a) + (a << 4 * b) for a, b in PAIRINGS[i])
            code -= (code >> 31) << 32
            choice = jnp.where(clash == 0, i, choice)
            partners = jnp.where(clash == 0, jnp.int32(code), partners)
        partner = lax.shift_right_logical(partners, 4 * home) & 15
        first_is_due = (home < partner) == own_due
        plan_ref[0] = choice
        plan_ref[1] = jnp.where(first_is_due, 0, 1)


def local_kernel(plan_ref, got_ref, bands_ref, turn_ref, out_ref):
    side = plan_ref[1]
    seq, _, _, q = got_ref.shape
    chans = out_ref.shape[2]
    length = 2 * seq * C8
    kept = turn_ref.shape[0]
    row_fwd = bands_ref.at[pl.ds(0, length), :]
    row_inv = bands_ref.at[pl.ds(length, length // 2), :]
    col = bands_ref.at[pl.ds(length + length // 2, 2 * q), :]
    ct, st = turn_ref[:, :q], turn_ref[:, q:]
    edge = jnp.zeros((C8, q), jnp.float32)
    wide = 2

    def narrow(value):
        return value.astype(jnp.bfloat16)

    def beside(values):
        return narrow(jnp.concatenate(values, 1))

    def below(values):
        return jnp.concatenate(values, 0)

    def rows_of(at, first, count):
        return got_ref[:, at, first : first + count, :].astype(jnp.float32).reshape(seq * count, q)

    def spectra(head):
        turned = []
        for i in range(wide):
            value = head[:, i * q : (i + 1) * q]
            re = value[:kept]
            im = below([edge, value[kept:], edge])
            turned.append(jnp.concatenate([re * ct + im * st, im * ct - re * st], 1))
        return dot(narrow(below(turned)), col[:, : 2 * q])

    out_ref[:, 1 - side, :, :] = jnp.zeros((seq, chans, q), jnp.bfloat16)
    for first in range(0, chans // C8, wide):
        taps, signal = [], []
        for group in range(first, first + wide):
            if group:
                taps.append(rows_of(1 - side, (group - 1) * 2 * C8, 2 * C8))
            else:
                taps.append(rows_of(side, chans, 2 * C8))
            signal.append(rows_of(side, group * C8, C8))
        filt = spectra(dot(row_fwd[...], beside(taps)))
        spec = spectra(dot(row_fwd[:, : seq * C8], beside(signal)))
        f_re, f_im, s_re, s_im = filt[:, :q], filt[:, q:], spec[:, :q], spec[:, q:]
        u = dot(beside([s_re * f_re - s_im * f_im, s_re * f_im + s_im * f_re]), col[:, 2 * q :])
        back = []
        for i in range(wide):
            u_re, u_im = u[i * kept : (i + 1) * kept, :q], u[i * kept : (i + 1) * kept, q:]
            v_im = u_re * st + u_im * ct
            back.append(below([u_re * ct - u_im * st, v_im[C8 : kept - C8]]))
        tail = dot(row_inv[...], beside(back))
        for i in range(wide):
            value = tail[:, i * q : (i + 1) * q].reshape(seq, C8, q)
            group = first + i
            out_ref[:, side, group * C8 : (group + 1) * C8, :] = narrow(value)


def exchange(choice, value, seq, reqs):
    def paired(pairs):
        groups = [[s * reqs + side for s in range(seq) for side in pair] for pair in pairs]
        return lambda x: lax.all_to_all(x, ("seq", "req"), split_axis=0, concat_axis=0, axis_index_groups=groups)

    return lax.switch(choice, [paired(pairs) for pairs in PAIRINGS], value)


def per_device(consts, context, filters, lengths):
    seq, reqs = lax.axis_size("seq"), lax.axis_size("req")
    home = lax.axis_index("req")
    q = context.shape[2]
    peers = 2 * seq
    chans = context.shape[1] // peers
    rows = chans + 2 * C8
    smem = pl.BlockSpec(memory_space=pltpu.SMEM)
    vmem = pl.BlockSpec(memory_space=pltpu.VMEM)

    steps = 2
    part = peers // steps
    sent, plan = pl.pallas_call(
        pack_kernel,
        out_shape=[jax.ShapeDtypeStruct((peers, rows, q), jnp.bfloat16), jax.ShapeDtypeStruct((2,), jnp.int32)],
        grid=(steps,),
        in_specs=[
            smem,
            smem,
            pl.BlockSpec((part, chans, q), lambda i: (i, 0, 0)),
            pl.BlockSpec((part, chans, 2 * q), lambda i: (i, 0, 0)),
        ],
        out_specs=[pl.BlockSpec((part, rows, q), lambda i: (i, 0, 0)), smem],
        name="pack",
    )(lengths, home[None], context.reshape(peers, chans, q), filters.reshape(peers, chans, 2 * q))
    got = exchange(plan[0], sent, seq, reqs)
    out = pl.pallas_call(
        local_kernel,
        out_shape=jax.ShapeDtypeStruct((seq, 2, chans, q), jnp.bfloat16),
        in_specs=[smem] + [vmem] * 3,
        out_specs=vmem,
        compiler_params=pltpu.CompilerParams(vmem_limit_bytes=48 << 20),
        name="transform",
    )(plan, got.reshape(seq, 2, rows, q), *consts)
    done = exchange(plan[0], out.reshape(peers, chans, q), seq, reqs)
    return done.reshape(context.shape)


def solution(mesh):
    seq = mesh.shape["seq"]
    consts = tables(2 * seq, B // seq)
    spec = P("req", "chan", "seq")
    return jax.shard_map(
        functools.partial(per_device, consts),
        mesh=mesh,
        in_specs=(spec, P("chan", "seq"), P()),
        out_specs=spec,
        check_vma=False,
    )
```

```python
import functools
import math

import jax
import jax.numpy as jnp
import numpy as np
from jax import lax
from jax.experimental import pallas as pl
from jax.experimental.pallas import tpu as pltpu
from jax.sharding import PartitionSpec as P

B = 4096
C8 = 8


def trig_pair(first_count, second_count, stride_len, full_len):
    left = np.arange(first_count)[:, None]
    right = np.arange(second_count)[None, :]
    phases = (left * right * stride_len) % full_len
    angles = phases.astype(np.float64) * (2.0 * math.pi / full_len)
    return np.cos(angles).astype(np.float32), np.sin(angles).astype(np.float32)


def tables(rows, cols):
    full = rows * cols
    half = rows // 2
    cp, sp = trig_pair(rows, rows, cols, full)
    ct, st = trig_pair(rows, cols, 1, full)
    cq, sq = trig_pair(cols, cols, rows, full)
    eye = np.eye(C8, dtype=np.float32)
    row_fwd = np.kron(np.concatenate([cp[: half + 1], -sp[1:half]], 0), eye)
    twice = np.where(np.arange(half + 1) % half == 0, 1.0, 2.0) / full
    back = np.concatenate([cp[half:, : half + 1] * twice, -sp[half:, 1:half] * twice[1:half]], 1)
    row_inv = np.kron(back, eye)
    col = np.concatenate([np.block([[cq, -sq], [sq, cq]]), np.block([[cq, sq], [-sq, cq]])], 1)
    bands = np.concatenate([row_fwd, row_inv, col], 0).astype(jnp.bfloat16)
    turn = np.repeat(np.concatenate([ct, st], 1)[: half + 1], C8, axis=0).astype(np.float32)
    return bands, turn


def dot(a, b):
    return jnp.dot(a, b, preferred_element_type=jnp.float32)


PAIRINGS = (
    ((0, 1), (2, 3), (4, 5), (6, 7)),
    ((0, 1), (2, 3), (4, 6), (5, 7)),
    ((0, 3), (1, 2), (4, 7), (5, 6)),
    ((0, 7), (1, 2), (3, 4), (5, 6)),
    ((0, 3), (1, 2), (4, 5), (6, 7)),
    ((0, 7), (1, 6), (2, 5), (3, 4)),
    ((0, 1), (2, 7), (3, 6), (4, 5)),
    ((0, 6), (1, 3), (2, 4), (5, 7)),
    ((0, 2), (1, 7), (3, 5), (4, 6)),
    ((0, 5), (1, 4), (2, 3), (6, 7)),
)


def pack_kernel(lengths_ref, home_ref, context_ref, filters_ref, sent_ref, plan_ref):
    reqs = lengths_ref.shape[0]
    chans = context_ref.shape[1]
    few = 2 * C8
    home = home_ref[0]

    own_due = lax.rem(lengths_ref[home], B) == 0

    @pl.when(own_due)
    def _():
        sent_ref[:, :chans, :] = context_ref[...]
        sent_ref[:, chans:, :] = filters_ref[:, :few, :]

    @pl.when(jnp.logical_not(own_due))
    def _():
        sent_ref[...] = filters_ref[:, few:, :]

    @pl.when(pl.program_id(0) == 0)
    def _():
        due = [jnp.where(lax.rem(lengths_ref[r], B) == 0, 1, 0) for r in range(reqs)]
        choice, partners = jnp.int32(0), jnp.int32(0)
        for i in reversed(range(len(PAIRINGS))):
            clash = functools.reduce(jnp.add, [due[a] * due[b] for a, b in PAIRINGS[i]])
            code = sum((b << 4 * a) + (a << 4 * b) for a, b in PAIRINGS[i])
            code -= (code >> 31) << 32
            choice = jnp.where(clash == 0, i, choice)
            partners = jnp.where(clash == 0, jnp.int32(code), partners)
        partner = lax.shift_right_logical(partners, 4 * home) & 15
        first_is_due = (home < partner) == own_due
        plan_ref[0] = choice
        plan_ref[1] = jnp.where(first_is_due, 0, 1)


def local_kernel(plan_ref, got_ref, bands_ref, turn_ref, out_ref):
    side = plan_ref[1]
    seq, _, _, q = got_ref.shape
    chans = out_ref.shape[2]
    length = 2 * seq * C8
    kept = turn_ref.shape[0]
    row_fwd = bands_ref.at[pl.ds(0, length), :]
    row_inv = bands_ref.at[pl.ds(length, length // 2), :]
    col = bands_ref.at[pl.ds(length + length // 2, 2 * q), :]
    ct, st = turn_ref[:, :q], turn_ref[:, q:]
    edge = jnp.zeros((C8, q), jnp.float32)
    wide = 2

    def narrow(value):
        return value.astype(jnp.bfloat16)

    def beside(values):
        return narrow(jnp.concatenate(values, 1))

    def below(values):
        return jnp.concatenate(values, 0)

    def rows_of(at, first, count):
        return got_ref[:, at, first : first + count, :].astype(jnp.float32).reshape(seq * count, q)

    def spectra(head):
        turned = []
        for i in range(wide):
            value = head[:, i * q : (i + 1) * q]
            re = value[:kept]
            im = below([edge, value[kept:], edge])
            turned.append(jnp.concatenate([re * ct + im * st, im * ct - re * st], 1))
        return dot(narrow(below(turned)), col[:, : 2 * q])

    out_ref[:, 1 - side, :, :] = jnp.zeros((seq, chans, q), jnp.bfloat16)
    for first in range(0, chans // C8, wide):
        taps, signal = [], []
        for group in range(first, first + wide):
            if group:
                taps.append(rows_of(1 - side, (group - 1) * 2 * C8, 2 * C8))
            else:
                taps.append(rows_of(side, chans, 2 * C8))
            signal.append(rows_of(side, group * C8, C8))
        filt = spectra(dot(row_fwd[...], beside(taps)))
        spec = spectra(dot(row_fwd[:, : seq * C8], beside(signal)))
        f_re, f_im, s_re, s_im = filt[:, :q], filt[:, q:], spec[:, :q], spec[:, q:]
        u = dot(beside([s_re * f_re - s_im * f_im, s_re * f_im + s_im * f_re]), col[:, 2 * q :])
        back = []
        for i in range(wide):
            u_re, u_im = u[i * kept : (i + 1) * kept, :q], u[i * kept : (i + 1) * kept, q:]
            v_im = u_re * st + u_im * ct
            back.append(below([u_re * ct - u_im * st, v_im[C8 : kept - C8]]))
        tail = dot(row_inv[...], beside(back))
        for i in range(wide):
            value = tail[:, i * q : (i + 1) * q].reshape(seq, C8, q)
            group = first + i
            out_ref[:, side, group * C8 : (group + 1) * C8, :] = narrow(value)


def exchange(choice, value, seq, reqs):
    def paired(pairs):
        groups = [[s * reqs + side for s in range(seq) for side in pair] for pair in pairs]
        return lambda x: lax.all_to_all(x, ("seq", "req"), split_axis=0, concat_axis=0, axis_index_groups=groups)

    return lax.switch(choice, [paired(pairs) for pairs in PAIRINGS], value)


def per_device(consts, context, filters, lengths):
    seq, reqs = lax.axis_size("seq"), lax.axis_size("req")
    home = lax.axis_index("req")
    q = context.shape[2]
    peers = 2 * seq
    chans = context.shape[1] // peers
    rows = chans + 2 * C8
    smem = pl.BlockSpec(memory_space=pltpu.SMEM)
    vmem = pl.BlockSpec(memory_space=pltpu.VMEM)

    halves = filters.reshape(peers, chans // C8, C8, 2, q).transpose(0, 1, 3, 2, 4).reshape(peers, 2 * chans, q)
    steps = 2
    part = peers // steps
    sent, plan = pl.pallas_call(
        pack_kernel,
        out_shape=[jax.ShapeDtypeStruct((peers, rows, q), jnp.bfloat16), jax.ShapeDtypeStruct((2,), jnp.int32)],
        grid=(steps,),
        in_specs=[
            smem,
            smem,
            pl.BlockSpec((part, chans, q), lambda i: (i, 0, 0)),
            pl.BlockSpec((part, 2 * chans, q), lambda i: (i, 0, 0)),
        ],
        out_specs=[pl.BlockSpec((part, rows, q), lambda i: (i, 0, 0)), smem],
        name="pack",
    )(lengths, home[None], context.reshape(peers, chans, q), halves)
    got = exchange(plan[0], sent, seq, reqs)
    out = pl.pallas_call(
        local_kernel,
        out_shape=jax.ShapeDtypeStruct((seq, 2, chans, q), jnp.bfloat16),
        in_specs=[smem] + [vmem] * 3,
        out_specs=vmem,
        compiler_params=pltpu.CompilerParams(vmem_limit_bytes=48 << 20),
        name="transform",
    )(plan, got.reshape(seq, 2, rows, q), *consts)
    done = exchange(plan[0], out.reshape(peers, chans, q), seq, reqs)
    return done.reshape(context.shape)


def solution(mesh):
    seq = mesh.shape["seq"]
    consts = tables(2 * seq, B // seq)
    spec = P("req", "chan", "seq")
    return jax.shard_map(
        functools.partial(per_device, consts),
        mesh=mesh,
        in_specs=(spec, P("chan", "seq"), P()),
        out_specs=spec,
        check_vma=False,
    )
```

```python
import functools
import math

import jax
import jax.numpy as jnp
import numpy as np
from jax import lax
from jax.experimental import pallas as pl
from jax.experimental.pallas import tpu as pltpu
from jax.sharding import PartitionSpec as P

B = 4096
C8 = 8


def trig_pair(first_count, second_count, stride_len, full_len):
    left = np.arange(first_count)[:, None]
    right = np.arange(second_count)[None, :]
    phases = (left * right * stride_len) % full_len
    angles = phases.astype(np.float64) * (2.0 * math.pi / full_len)
    return np.cos(angles).astype(np.float32), np.sin(angles).astype(np.float32)


def tables(rows, cols):
    full = rows * cols
    half = rows // 2
    cp, sp = trig_pair(rows, rows, cols, full)
    ct, st = trig_pair(rows, cols, 1, full)
    cq, sq = trig_pair(cols, cols, rows, full)
    eye = np.eye(C8, dtype=np.float32)
    row_fwd = np.kron(np.concatenate([cp[: half + 1], -sp[1:half]], 0), eye)
    twice = np.where(np.arange(half + 1) % half == 0, 1.0, 2.0) / full
    back = np.concatenate([cp[half:, : half + 1] * twice, -sp[half:, 1:half] * twice[1:half]], 1)
    row_inv = np.kron(back, eye)
    col = np.concatenate([np.block([[cq, -sq], [sq, cq]]), np.block([[cq, sq], [-sq, cq]])], 1)
    bands = np.concatenate([row_fwd, row_inv, col], 0).astype(jnp.bfloat16)
    turn = np.repeat(np.concatenate([ct, st], 1)[: half + 1], C8, axis=0).astype(np.float32)
    return bands, turn


def dot(a, b):
    return jnp.dot(a, b, preferred_element_type=jnp.float32)


PAIRINGS = (
    ((0, 1), (2, 3), (4, 5), (6, 7)),
    ((0, 1), (2, 3), (4, 6), (5, 7)),
    ((0, 3), (1, 2), (4, 7), (5, 6)),
    ((0, 7), (1, 2), (3, 4), (5, 6)),
    ((0, 3), (1, 2), (4, 5), (6, 7)),
    ((0, 7), (1, 6), (2, 5), (3, 4)),
    ((0, 1), (2, 7), (3, 6), (4, 5)),
    ((0, 6), (1, 3), (2, 4), (5, 7)),
    ((0, 2), (1, 7), (3, 5), (4, 6)),
    ((0, 5), (1, 4), (2, 3), (6, 7)),
)


def pack_kernel(lengths_ref, home_ref, context_ref, filters_ref, sent_ref, plan_ref):
    reqs = lengths_ref.shape[0]
    chans = context_ref.shape[1]
    few = 2 * C8
    home = home_ref[0]

    own_due = lax.rem(lengths_ref[home], B) == 0

    @pl.when(own_due)
    def _():
        sent_ref[:, :chans, :] = context_ref[...]
        sent_ref[:, chans:, :] = filters_ref[:, :few, :]

    @pl.when(jnp.logical_not(own_due))
    def _():
        sent_ref[...] = filters_ref[:, few:, :]

    @pl.when(pl.program_id(0) == 0)
    def _():
        due = [jnp.where(lax.rem(lengths_ref[r], B) == 0, 1, 0) for r in range(reqs)]
        choice, partners = jnp.int32(0), jnp.int32(0)
        for i in reversed(range(len(PAIRINGS))):
            clash = functools.reduce(jnp.add, [due[a] * due[b] for a, b in PAIRINGS[i]])
            code = sum((b << 4 * a) + (a << 4 * b) for a, b in PAIRINGS[i])
            code -= (code >> 31) << 32
            choice = jnp.where(clash == 0, i, choice)
            partners = jnp.where(clash == 0, jnp.int32(code), partners)
        partner = lax.shift_right_logical(partners, 4 * home) & 15
        first_is_due = (home < partner) == own_due
        plan_ref[0] = choice
        plan_ref[1] = jnp.where(first_is_due, 0, 1)


def local_kernel(plan_ref, got_ref, bands_ref, turn_ref, out_ref):
    side = plan_ref[1]
    seq, _, _, q = got_ref.shape
    chans = out_ref.shape[2]
    length = 2 * seq * C8
    kept = turn_ref.shape[0]
    row_fwd = bands_ref.at[pl.ds(0, length), :]
    row_inv = bands_ref.at[pl.ds(length, length // 2), :]
    col = bands_ref.at[pl.ds(length + length // 2, 2 * q), :]
    ct, st = turn_ref[:, :q], turn_ref[:, q:]
    edge = jnp.zeros((C8, q), jnp.float32)
    wide = 4

    def narrow(value):
        return value.astype(jnp.bfloat16)

    def beside(values):
        return narrow(jnp.concatenate(values, 1))

    def below(values):
        return jnp.concatenate(values, 0)

    def rows_of(at, first, count):
        return got_ref[:, at, first : first + count, :].astype(jnp.float32).reshape(seq * count, q)

    def spectra(head):
        turned = []
        for i in range(wide):
            value = head[:, i * q : (i + 1) * q]
            re = value[:kept]
            im = below([edge, value[kept:], edge])
            turned.append(jnp.concatenate([re * ct + im * st, im * ct - re * st], 1))
        return dot(narrow(below(turned)), col[:, : 2 * q])

    out_ref[:, 1 - side, :, :] = jnp.zeros((seq, chans, q), jnp.bfloat16)
    for first in range(0, chans // C8, wide):
        taps, signal = [], []
        for group in range(first, first + wide):
            if group:
                taps.append(rows_of(1 - side, (group - 1) * 2 * C8, 2 * C8))
            else:
                taps.append(rows_of(side, chans, 2 * C8))
            signal.append(rows_of(side, group * C8, C8))
        filt = spectra(dot(row_fwd[...], beside(taps)))
        spec = spectra(dot(row_fwd[:, : seq * C8], beside(signal)))
        f_re, f_im, s_re, s_im = filt[:, :q], filt[:, q:], spec[:, :q], spec[:, q:]
        u = dot(beside([s_re * f_re - s_im * f_im, s_re * f_im + s_im * f_re]), col[:, 2 * q :])
        back = []
        for i in range(wide):
            u_re, u_im = u[i * kept : (i + 1) * kept, :q], u[i * kept : (i + 1) * kept, q:]
            v_im = u_re * st + u_im * ct
            back.append(below([u_re * ct - u_im * st, v_im[C8 : kept - C8]]))
        tail = dot(row_inv[...], beside(back))
        for i in range(wide):
            value = tail[:, i * q : (i + 1) * q].reshape(seq, C8, q)
            group = first + i
            out_ref[:, side, group * C8 : (group + 1) * C8, :] = narrow(value)


def exchange(choice, value, seq, reqs):
    def paired(pairs):
        groups = [[s * reqs + side for s in range(seq) for side in pair] for pair in pairs]
        return lambda x: lax.all_to_all(x, ("seq", "req"), split_axis=0, concat_axis=0, axis_index_groups=groups)

    return lax.switch(choice, [paired(pairs) for pairs in PAIRINGS], value)


def per_device(consts, context, filters, lengths):
    seq, reqs = lax.axis_size("seq"), lax.axis_size("req")
    home = lax.axis_index("req")
    q = context.shape[2]
    peers = 2 * seq
    chans = context.shape[1] // peers
    rows = chans + 2 * C8
    smem = pl.BlockSpec(memory_space=pltpu.SMEM)
    vmem = pl.BlockSpec(memory_space=pltpu.VMEM)

    halves = filters.reshape(peers, chans // C8, C8, 2, q).transpose(0, 1, 3, 2, 4).reshape(peers, 2 * chans, q)
    steps = 2
    part = peers // steps
    sent, plan = pl.pallas_call(
        pack_kernel,
        out_shape=[jax.ShapeDtypeStruct((peers, rows, q), jnp.bfloat16), jax.ShapeDtypeStruct((2,), jnp.int32)],
        grid=(steps,),
        in_specs=[
            smem,
            smem,
            pl.BlockSpec((part, chans, q), lambda i: (i, 0, 0)),
            pl.BlockSpec((part, 2 * chans, q), lambda i: (i, 0, 0)),
        ],
        out_specs=[pl.BlockSpec((part, rows, q), lambda i: (i, 0, 0)), smem],
        name="pack",
    )(lengths, home[None], context.reshape(peers, chans, q), halves)
    got = exchange(plan[0], sent, seq, reqs)
    out = pl.pallas_call(
        local_kernel,
        out_shape=jax.ShapeDtypeStruct((seq, 2, chans, q), jnp.bfloat16),
        in_specs=[smem] + [vmem] * 3,
        out_specs=vmem,
        compiler_params=pltpu.CompilerParams(vmem_limit_bytes=48 << 20),
        name="transform",
    )(plan, got.reshape(seq, 2, rows, q), *consts)
    done = exchange(plan[0], out.reshape(peers, chans, q), seq, reqs)
    return done.reshape(context.shape)


def solution(mesh):
    seq = mesh.shape["seq"]
    consts = tables(2 * seq, B // seq)
    spec = P("req", "chan", "seq")
    return jax.shard_map(
        functools.partial(per_device, consts),
        mesh=mesh,
        in_specs=(spec, P("chan", "seq"), P()),
        out_specs=spec,
        check_vma=False,
    )
```
